768 devices in a mesh: dp: 192 (over y, z, core), expert: 4 (over x).
Axes of the slice: x: 4, y: 8, z: 12, core: 2. Of those that a mesh axis runs over, the one named last changes fastest.
Arguments:
- tokens: bfloat16 [128, 6144], P('expert', 'dp'), may hold values from -6 to 6
- routes: int32 [128, 2], P('expert'), may hold values from 0 to 3, all different within a row; in each aligned block of 32 rows (0 to 31, 32 to 63, ...) at most 24 rows name the same one
- probs: float32 [128, 2], P('expert'), may hold values from 0.1 to 0.9
- w_gate: bfloat16 [4, 12288, 6144], P('expert', 'dp'), may hold values from -0.078125 to 0.078125
- w_up: bfloat16 [4, 12288, 6144], P('expert', 'dp'), may hold values from -0.078125 to 0.078125
- w_down: bfloat16 [4, 12288, 6144], P('expert', 'dp'), may hold values from -0.0546875 to 0.0546875
- grad_out: bfloat16 [128, 6144], P('expert', 'dp'), may hold values from -6 to 6
Outputs:
- mixed: bfloat16 [128, 6144], P('expert', 'dp')
- grad_tokens: bfloat16 [128, 6144], P('expert', 'dp')
- grad_gate: bfloat16 [4, 12288, 6144], P('expert', 'dp')
- grad_up: bfloat16 [4, 12288, 6144], P('expert', 'dp')
- grad_down: bfloat16 [4, 12288, 6144], P('expert', 'dp')
The draws below stay inside these ranges and needn't reach their ends.
Inputs may be any that keep to these rules, and one draw needn't show every extreme that they name: `routes`: each row names 2 different experts; within the rows of one index of expert (aligned blocks of 32 rows) no expert is named by more than 24 rows, and in some block one expert is named by exactly 24.
All inputs are finite; a program needn't handle non-finite values.
Results may differ from the reference program's by a relative error of at most 0.01.
Values may be sent and summed in bfloat16 or wider, within the bound.
No kernel may reach another device: no remote copies, remote signals or barrier semaphores. Data moves between devices by JAX's collectives and lax.ppermute only.
A program may use at most 32 MiB of HBM per device.

```python
import math
import jax
import jax.numpy as jnp
import numpy as np
from jax import lax

D = 6144
TOK_DEV = 32
TOP = 2
EXPERTS = 4
FF = 12288
TOKENS = 128
CAP = 24


def block_scale(own_key, shape, pieces, smallest, high):
    def one(position, shards_of):
        heights = jax.random.uniform(jax.random.fold_in(jax.random.fold_in(own_key, 6), position), (shards_of,), jnp.float32, smallest / len(pieces), high / len(pieces))
        return jnp.repeat(jnp.exp(heights), shape[position] // shards_of).reshape((-1,) + (1,) * (len(shape) - position - 1))

    factor_of = one(*pieces[0])
    for cut in pieces[1:]:
        factor_of = factor_of * one(*cut)
    return factor_of


def shared_out(key, own, number, rows, number_of, top, most, skew):
    sequence = jax.random.permutation(key, number_of)
    crowded, common = shares(number_of, rows * top, most, skew, True), shares(number_of, rows * top, most, skew, False)
    places = jnp.arange(number_of)

    def named(tallies, offset_by):
        used = int((tallies > 0).sum())
        fixed = max(1, used // 4)
        moved = fixed + (places - fixed + offset_by * (used - fixed)) % max(1, number_of - fixed)
        return jnp.zeros((number_of,), jnp.int32).at[sequence[jnp.where(places < fixed, places, moved)]].set(jnp.asarray(tallies, jnp.int32))

    tallies = jnp.where(number % 4 == 0, named(crowded, number // 4), named(common, number - number // 4 - 1))
    mixed = jax.random.permutation(jax.random.fold_in(own, 3), number_of)
    source_of, sink = mixed[0:number_of // 2 * 2:2], mixed[1:number_of // 2 * 2:2]
    slack = jnp.minimum(tallies[source_of] - 1, most - tallies[sink]) // 2
    slack = jnp.where((source_of == sequence[0]) | (sink == sequence[0]) | (tallies[sink] == 0), 0, jnp.maximum(slack, 0))
    moved = jax.random.randint(jax.random.fold_in(own, 4), (number_of // 2,), 0, 1 << 20) % (slack + 1)
    tallies = tallies.at[source_of].add(-moved).at[sink].add(moved)
    labels = jnp.searchsorted(jnp.cumsum(tallies), jnp.arange(rows * top), side="right").astype(jnp.int32)
    grid = labels.reshape(top, rows).T
    grid = grid[jax.random.permutation(jax.random.fold_in(own, 1), rows)]
    offset_by = jax.random.randint(jax.random.fold_in(own, 2), (rows, 1), 0, top)
    return jnp.take_along_axis(grid, (jnp.arange(top)[None, :] + offset_by) % top, axis=1)


def shares(count, total, reach, slope, full):
    portions = [(1 << 20) // math.isqrt(rank ** slope) + 1 for rank in range(1, count + 1)]
    largest = reach if full else min(reach, max(-(-total // count), total * portions[0] // sum(portions)))
    least = 1 if total - largest >= count - 1 else 0
    given, surplus = [largest] + [least] * (count - 1), total - largest - least * (count - 1)
    while surplus > 0:
        movable = [i for i in range(1, count) if given[i] < largest] or [i for i in range(1, count) if given[i] < reach]
        mass, remaining = sum([portions[i] for i in movable]), surplus
        for i in movable:
            addition = min(reach - given[i], max(1, remaining * portions[i] // mass), surplus)
            given[i] = given[i] + addition
            surplus = surplus - addition
    return np.array(given)


def normal_values(own_key, dims, deviation, reach, pieces=(), dtype=jnp.bfloat16):
    entries = deviation * jax.random.normal(own_key, dims, jnp.float32)
    if pieces:
        entries = entries * block_scale(own_key, dims, pieces, -0.22, 0.18)
    return jnp.clip(entries, -reach, reach).astype(dtype)


def setup_inputs(seed: int = 0) -> dict:
    keys = jax.random.split(jax.random.key(seed), 8)
    tokens = normal_values(keys[0], (TOKENS, D), 1.0, 6.0, ((0, 4), (1, 192)))
    routes_keys = jax.random.split(jax.random.fold_in(keys[1], 1), TOKENS // TOK_DEV)
    routes_turns = jax.random.permutation(jax.random.fold_in(keys[1], 3), TOKENS // TOK_DEV)
    routes = jax.vmap(lambda own, number: shared_out(jax.random.fold_in(keys[1], 2), own, number, TOK_DEV, EXPERTS, TOP, CAP, 1))(routes_keys, routes_turns).reshape((TOKENS, TOP))
    probs = jnp.clip(0.1 + 0.79999997 * jax.random.uniform(keys[2], (TOKENS, TOP), jnp.float32) ** block_scale(keys[2], (TOKENS, TOP), ((0, 4),), -0.2, 0.2), 0.1, 0.9)
    w_gate = normal_values(keys[3], (EXPERTS, FF, D), D ** -0.5, 0.078125, ((0, 4), (1, 192)))
    w_up = normal_values(keys[4], (EXPERTS, FF, D), D ** -0.5, 0.078125, ((0, 4), (1, 192)))
    w_down = normal_values(keys[5], (EXPERTS, FF, D), FF ** -0.5, 0.0546875, ((0, 4), (1, 192)))
    grad_out = normal_values(keys[6], (TOKENS, D), 1.0, 6.0, ((0, 4), (1, 192)))
    return dict(tokens=tokens, routes=routes, probs=probs, w_gate=w_gate, w_up=w_up, w_down=w_down, grad_out=grad_out)


def tdot(a, b):
    return lax.dot_general(a, b, (((0,), (0,)), ((), ())), preferred_element_type=jnp.float32)


def ndot(a, b):
    return lax.dot_general(a, b, (((1,), (1,)), ((), ())), preferred_element_type=jnp.float32)


def reference(tokens, routes, probs, w_gate, w_up, w_down, grad_out):
    mixed_sum = jnp.zeros(tokens.shape, jnp.float32)
    back_total = jnp.zeros(tokens.shape, jnp.float32)
    grads_gate = []
    grads_up = []
    grads_down = []
    for expert in range(EXPERTS):
        hits = routes == expert
        mask = jnp.sum(hits.astype(jnp.float32), axis=1)
        share = jnp.sum(jnp.where(hits, probs, 0.0), axis=1)
        rows = jnp.where(mask[:, None] > 0.5, tokens, jnp.zeros_like(tokens))
        gate = ndot(rows, w_gate[expert])
        upper = ndot(rows, w_up[expert])
        sig = jax.nn.sigmoid(gate)
        act = gate * sig
        hidden = (act * upper).astype(jnp.bfloat16)
        out_e = jnp.dot(hidden, w_down[expert], preferred_element_type=jnp.float32).astype(jnp.bfloat16)
        mixed_sum = mixed_sum + share[:, None] * out_e.astype(jnp.float32)
        cot = (share[:, None] * grad_out.astype(jnp.float32)).astype(jnp.bfloat16)
        grads_down.append(tdot(hidden, cot).astype(jnp.bfloat16))
        dhid = ndot(cot, w_down[expert])
        dgate = (dhid * upper * sig * (1.0 + gate * (1.0 - sig))).astype(jnp.bfloat16)
        dup = (dhid * act).astype(jnp.bfloat16)
        grads_gate.append(tdot(dgate, rows).astype(jnp.bfloat16))
        grads_up.append(tdot(dup, rows).astype(jnp.bfloat16))
        back_e = (jnp.dot(dgate, w_gate[expert], preferred_element_type=jnp.float32)
                  + jnp.dot(dup, w_up[expert], preferred_element_type=jnp.float32)).astype(jnp.bfloat16)
        back_total = back_total + back_e.astype(jnp.float32)
    return (mixed_sum.astype(jnp.bfloat16), back_total.astype(jnp.bfloat16),
            jnp.stack(grads_gate), jnp.stack(grads_up), jnp.stack(grads_down))
```

```python
import jax
import jax.numpy as jnp
from jax import lax
from jax.sharding import Mesh, PartitionSpec as P

CORES = 2
COLUMNS = 8
SLOTS = 24


def tdot(a, b):
    return lax.dot_general(a, b, (((0,), (0,)), ((), ())), preferred_element_type=jnp.float32)


def ndot(a, b):
    return lax.dot_general(a, b, (((1,), (1,)), ((), ())), preferred_element_type=jnp.float32)


def swap(a, axis):
    return lax.all_to_all(a, axis, split_axis=0, concat_axis=0, tiled=True)


def on_device(tokens, routes, probs, w_gate, w_up, w_down, grad_out):
    bf16, f32 = jnp.bfloat16, jnp.float32
    experts = lax.axis_size("expert")
    depth = lax.axis_size("z")
    columns = lax.axis_size("y")
    cores = lax.axis_size("core")
    first = lax.axis_index("core") == 0
    count, narrow = tokens.shape
    wide = depth * cores * narrow
    width = columns * wide
    rows_of = experts * SLOTS

    labels = lax.broadcasted_iota(jnp.int32, (experts, count, routes.shape[1]), 0)
    hits = routes[None] == labels
    mask = jnp.any(hits, axis=2)
    share = jnp.sum(jnp.where(hits, probs[None], 0.0), axis=2)
    earlier = lax.broadcasted_iota(jnp.int32, (count, count), 1) < lax.broadcasted_iota(jnp.int32, (count, count), 0)
    place = jnp.sum(jnp.where(earlier[None] & mask[:, None, :], 1, 0), axis=2)
    slots = lax.broadcasted_iota(jnp.int32, (experts, SLOTS, count), 1)
    chosen = (place[:, None, :] == slots) & mask[:, None, :]
    pick = chosen.reshape(rows_of, count).astype(bf16)
    weight = jnp.where(first, jnp.ones_like(share), share)
    slot_weight = jnp.sum(jnp.where(chosen, weight[:, None, :], 0.0), axis=2).reshape(rows_of, 1)

    both = jnp.stack([tokens, grad_out]).reshape(1, cores, count * narrow // 128, 128)
    sent = jnp.broadcast_to(both, (depth,) + both.shape[1:]).reshape(depth * cores, -1, 128)
    got = swap(sent, ("z", "core")).reshape(depth * cores, count, narrow)
    mine = got.transpose(1, 0, 2).reshape(count, wide)

    packed = (jnp.dot(pick, mine, preferred_element_type=f32) * slot_weight).astype(bf16)
    sent = jnp.broadcast_to(packed.reshape(1, experts, SLOTS, wide), (columns, experts, SLOTS, wide))
    got = swap(sent.reshape(columns * experts, SLOTS, wide), ("y", "expert"))
    mine = got.reshape(columns, rows_of, wide).transpose(1, 0, 2).reshape(rows_of, width)
    other = lax.ppermute(mine, "core", [(0, 1), (1, 0)])
    rows = jnp.where(first, mine, other)
    cot = jnp.where(first, other, mine)

    gate_w, up_w, down_w = w_gate[0], w_up[0], w_down[0]
    hidden_count = gate_w.shape[0]
    gate = ndot(rows, gate_w)
    upper = ndot(rows, up_w)
    dhid = ndot(cot, down_w)
    sig = jax.nn.sigmoid(gate)
    act = gate * sig
    hidden = (act * upper).astype(bf16)
    dgate = (dhid * upper * sig * (1.0 + gate * (1.0 - sig))).astype(bf16)
    dup = (dhid * act).astype(bf16)
    part_out = jnp.dot(hidden, down_w, preferred_element_type=f32)
    part_back = jnp.dot(dgate, gate_w, preferred_element_type=f32) + jnp.dot(dup, up_w, preferred_element_type=f32)

    away = jnp.where(first, part_back, part_out).astype(bf16)
    kept = jnp.where(first, part_out, part_back)
    total = (kept + lax.ppermute(away, "core", [(0, 1), (1, 0)]).astype(f32)).astype(bf16)
    sent = total.reshape(rows_of, columns, wide).transpose(1, 0, 2).reshape(columns * experts, SLOTS, wide)
    got = swap(sent, ("y", "expert")).reshape(columns, experts, SLOTS, wide)
    summed = jnp.sum(got.astype(f32), axis=0)
    back_weight = jnp.where(first, share, mask.astype(f32))
    spread = jnp.where(chosen, back_weight[:, None, :], 0.0).reshape(rows_of, count)
    placed = lax.dot_general(
        spread, summed.reshape(rows_of, wide), (((0,), (0,)), ((), ())),
        precision=lax.Precision.HIGHEST, preferred_element_type=f32,
    ).astype(bf16)
    sent = placed.reshape(count, depth * cores, narrow).transpose(1, 0, 2).reshape(depth * cores, -1, 128)
    got = swap(sent, ("z", "core")).reshape(depth, cores, count, narrow)
    result = jnp.sum(got.astype(f32), axis=0).astype(bf16)

    grad_down = tdot(hidden, cot).astype(bf16)
    paired = tdot(jnp.concatenate([dgate, dup], axis=1), rows)
    grad_gate = paired[:hidden_count].astype(bf16)
    grad_up = paired[hidden_count:].astype(bf16)
    return (result[0], result[1], grad_gate[None], grad_up[None], grad_down[None])


def solution(mesh):
    shape = mesh.devices.shape
    split = mesh.devices.reshape(COLUMNS, shape[0] // (COLUMNS * CORES), CORES, shape[1])
    fine = Mesh(split, ("y", "z", "core", "expert"))
    dp = ("y", "z", "core")
    placed = (
        P("expert", dp),
        P("expert", None),
        P("expert", None),
        P("expert", dp, None),
        P("expert", dp, None),
        P("expert", dp, None),
        P("expert", dp),
    )
    return jax.shard_map(
        on_device,
        mesh=fine,
        in_specs=placed,
        out_specs=(P("expert", dp), P("expert", dp), P("expert", dp, None), P("expert", dp, None), P("expert", dp, None)),
        check_vma=False,
    )
```

```python
import jax
import jax.numpy as jnp
from jax import lax
from jax.experimental import pallas as pl
from jax.experimental.pallas import tpu as pltpu
from jax.sharding import Mesh, PartitionSpec as P

CORES = 2
COLUMNS = 8
PAIR = 2
SLOTS = 24
HALF = 64
LANES = 128
ROOM = 40 * 1024 * 1024

bf16, f32 = jnp.bfloat16, jnp.float32


def tdot(a, b):
    return lax.dot_general(a, b, (((0,), (0,)), ((), ())), preferred_element_type=f32)


def ndot(a, b):
    return lax.dot_general(a, b, (((1,), (1,)), ((), ())), preferred_element_type=f32)


def swap(a, axis):
    return lax.all_to_all(a, axis, split_axis=0, concat_axis=0, tiled=True)


def across(a):
    return lax.ppermute(a, "core", [(0, 1), (1, 0)])


def cross(a, b):
    return (
        jnp.concatenate([a[:, :HALF], b[:, :HALF]], axis=1),
        jnp.concatenate([a[:, HALF:], b[:, HALF:]], axis=1),
    )


def tiles(width):
    per = width // (COLUMNS * 2 * LANES)
    for y in range(COLUMNS):
        for j in range(per):
            yield (y * per + j) * 2 * LANES, (y % PAIR) * PAIR, ((y // PAIR) * per + j) * LANES


def arrange(core_ref, gate_ref, up_ref, down_ref, keep_ref, send_ref):
    units = gate_ref.shape[0]

    def fill(pair_ref, single_ref):
        for at, place, to in tiles(gate_ref.shape[1]):
            a, b = slice(at, at + LANES), slice(at + LANES, at + 2 * LANES)
            for row, ref in ((0, gate_ref), (units, up_ref)):
                for zl, tile in enumerate(cross(ref[:, a], ref[:, b])):
                    pair_ref[place + zl, row:row + units, to:to + LANES] = tile
            for zl, tile in enumerate(cross(down_ref[:, a], down_ref[:, b])):
                single_ref[place + zl, 0:units, to:to + LANES] = tile
                single_ref[place + zl, units:2 * units, to:to + LANES] = tile

    @pl.when(core_ref[0] == 0)
    def _():
        fill(keep_ref, send_ref)

    @pl.when(core_ref[0] != 0)
    def _():
        fill(send_ref, keep_ref)


def project(mine_ref, keep_ref, recv_ref, out_ref):
    n = keep_ref.shape[1]
    for part, ref in ((0, keep_ref), (1, recv_ref)):
        total = ndot(mine_ref[0], ref[0])
        for b in range(1, mine_ref.shape[0]):
            total = total + ndot(mine_ref[b], ref[b])
        out_ref[:, part * n:(part + 1) * n] = total


def expand(core_ref, mine_ref, other_ref, keep_ref, recv_ref, part_ref, hidden_ref, pair_ref):
    units = hidden_ref.shape[1]
    first = core_ref[0] == 0
    mine, other = mine_ref[...], other_ref[...]
    own_front, far_front = mine[:, :2 * units], mine[:, 2 * units:]
    own_back, far_back = other[:, 2 * units:], other[:, :2 * units]
    sides = []
    for here, there in ((own_front, own_back), (far_front, far_back)):
        proj = jnp.where(first, here, there)
        dhid = jnp.where(first, there, here)[:, :units]
        gate, upper = proj[:, :units], proj[:, units:]
        sig = jax.nn.sigmoid(gate)
        act = gate * sig
        hidden = (act * upper).astype(bf16)
        dgate = (dhid * upper * sig * (1.0 + gate * (1.0 - sig))).astype(bf16)
        dup = (dhid * act).astype(bf16)
        sides.append((hidden, jnp.concatenate([dgate, dup], axis=1)))
    hidden_ref[...] = sides[0][0]
    pair_ref[...] = sides[0][1]
    lefts = []
    for hidden, pair in sides:
        lone = jnp.concatenate([hidden, jnp.zeros_like(hidden)], axis=1)
        lefts.append(jnp.where(first, pair.astype(f32), lone.astype(f32)).astype(bf16))
    for b in range(keep_ref.shape[0]):
        total = jnp.dot(lefts[0], keep_ref[b], preferred_element_type=f32)
        total = total + jnp.dot(lefts[1], recv_ref[b], preferred_element_type=f32)
        part_ref[b] = total.astype(bf16)


def weigh(core_ref, mine_ref, other_ref, hidden_ref, pair_ref, gate_ref, up_ref, down_ref):
    units = hidden_ref.shape[1]

    def fill(rows_ref, cot_ref):
        hidden, pair = hidden_ref[...], pair_ref[...]
        for at, place, to in tiles(gate_ref.shape[1]):
            both = []
            for ref in (rows_ref, cot_ref):
                both.append(jnp.concatenate(cross(ref[place, :, to:to + LANES], ref[place + 1, :, to:to + LANES]), axis=1))
            grads = tdot(pair, both[0]).astype(bf16)
            gate_ref[:, at:at + 2 * LANES] = grads[:units]
            up_ref[:, at:at + 2 * LANES] = grads[units:]
            down_ref[:, at:at + 2 * LANES] = tdot(hidden, both[1]).astype(bf16)

    @pl.when(core_ref[0] == 0)
    def _():
        fill(mine_ref, other_ref)

    @pl.when(core_ref[0] != 0)
    def _():
        fill(other_ref, mine_ref)


def kernel(body, outs, cost, core, *arrays):
    specs = [pl.BlockSpec(memory_space=pltpu.VMEM)] * len(arrays)
    if core is not None:
        specs, arrays = [pl.BlockSpec(memory_space=pltpu.SMEM)] + specs, (core,) + arrays
    return pl.pallas_call(
        body,
        out_shape=tuple(jax.ShapeDtypeStruct(s, d) for s, d in outs),
        in_specs=specs,
        out_specs=tuple(pl.BlockSpec(memory_space=pltpu.VMEM) for _ in outs),
        compiler_params=pltpu.CompilerParams(vmem_limit_bytes=ROOM),
        cost_estimate=pl.CostEstimate(flops=cost[0], bytes_accessed=cost[1], transcendentals=0),
        name=body.__name__,
    )(*arrays)


def on_device(tokens, routes, probs, w_gate, w_up, w_down, grad_out):
    experts = lax.axis_size("expert")
    cells = lax.axis_size("yh") * lax.axis_size("zh")
    near = PAIR * PAIR
    core = lax.axis_index("core")
    first = core == 0
    flag = core.astype(jnp.int32).reshape(1)
    count, narrow = tokens.shape
    wide = cells * CORES * narrow
    rows_of = experts * SLOTS
    units, width = w_gate.shape[1:]

    labels = lax.broadcasted_iota(jnp.int32, (experts, count, routes.shape[1]), 0)
    hits = routes[None] == labels
    mask = jnp.any(hits, axis=2)
    share = jnp.sum(jnp.where(hits, probs[None], 0.0), axis=2)
    earlier = lax.broadcasted_iota(jnp.int32, (count, count), 1) < lax.broadcasted_iota(jnp.int32, (count, count), 0)
    place = jnp.sum(jnp.where(earlier[None] & mask[:, None, :], 1, 0), axis=2)
    slots = lax.broadcasted_iota(jnp.int32, (experts, SLOTS, count), 1)
    chosen = (place[:, None, :] == slots) & mask[:, None, :]
    pick = chosen.reshape(rows_of, count).astype(bf16)
    weight = jnp.where(first, jnp.ones_like(share), share)
    slot_weight = jnp.sum(jnp.where(chosen, weight[:, None, :], 0.0), axis=2).reshape(rows_of, 1)

    both = jnp.stack([tokens, grad_out]).reshape(1, CORES, count * narrow // LANES, LANES)
    sent = jnp.broadcast_to(both, (cells,) + both.shape[1:]).reshape(cells * CORES, -1, LANES)
    got = swap(sent, ("yh", "zh", "core")).reshape(cells * CORES, count, narrow)
    local = got.transpose(1, 0, 2).reshape(count, wide)

    big = 2 * units * width
    keep, send = kernel(
        arrange, [((near, 2 * units, wide), bf16)] * 2, (0, 8 * big), flag, w_gate[0], w_up[0], w_down[0]
    )
    recv = across(send)

    packed = (jnp.dot(pick, local, preferred_element_type=f32) * slot_weight).astype(bf16)
    sent = jnp.broadcast_to(packed.reshape(1, experts, SLOTS, wide), (near, experts, SLOTS, wide))
    got = swap(sent.reshape(near * experts, SLOTS, wide), ("yl", "zl", "expert"))
    mine = got.reshape(near, rows_of, wide)

    work = 2 * rows_of * 2 * big
    (proj,) = kernel(project, [((rows_of, 4 * units), f32)], (work, 6 * big), None, mine, keep, recv)
    part, hidden, pair = kernel(
        expand,
        [((near, rows_of, wide), bf16), ((rows_of, units), bf16), ((rows_of, 2 * units), bf16)],
        (work, 6 * big), flag, proj, across(proj), keep, recv,
    )

    got = swap(part.reshape(near * experts, SLOTS, wide), ("yl", "zl", "expert"))
    summed = jnp.sum(got.reshape(near, rows_of, wide).astype(f32), axis=0)
    back_weight = jnp.where(first, mask.astype(f32), share)
    spread = jnp.where(chosen, back_weight[:, None, :], 0.0).reshape(rows_of, count)
    placed = lax.dot_general(
        spread, summed, (((0,), (0,)), ((), ())), precision=lax.Precision.HIGHEST, preferred_element_type=f32
    ).astype(bf16)
    sent = placed.reshape(count, cells * CORES, narrow).transpose(1, 0, 2).reshape(cells * CORES, -1, LANES)
    got = swap(sent, ("yh", "zh", "core")).reshape(cells, CORES, count, narrow)
    result = jnp.sum(got.astype(f32), axis=0).astype(bf16)

    mine, part = lax.optimization_barrier((mine, part))
    grad_gate, grad_up, grad_down = kernel(
        weigh, [((units, width), bf16)] * 3, (work, 8 * big), flag, mine, across(mine), hidden, pair
    )
    return (result[1], result[0], grad_gate[None], grad_up[None], grad_down[None])


def solution(mesh):
    dp, experts = mesh.devices.shape
    depth = dp // (COLUMNS * CORES)
    split = mesh.devices.reshape(COLUMNS // PAIR, PAIR, depth // PAIR, PAIR, CORES, experts)
    fine = Mesh(split, ("yh", "yl", "zh", "zl", "core", "expert"))
    dp = ("yh", "yl", "zh", "zl", "core")
    placed = (
        P("expert", dp),
        P("expert", None),
        P("expert", None),
        P("expert", dp, None),
        P("expert", dp, None),
        P("expert", dp, None),
        P("expert", dp),
    )
    return jax.shard_map(
        on_device,
        mesh=fine,
        in_specs=placed,
        out_specs=(P("expert", dp), P("expert", dp), P("expert", dp, None), P("expert", dp, None), P("expert", dp, None)),
        check_vma=False,
    )
```

```python
import jax
import jax.numpy as jnp
from jax import lax
from jax.experimental import pallas as pl
from jax.experimental.pallas import tpu as pltpu
from jax.sharding import Mesh, PartitionSpec as P

CORES = 2
COLUMNS = 8
PAIR = 2
SLOTS = 24
HALF = 64
LANES = 128
ROOM = 16 * 1024 * 1024
ALL = 60 * 1024 * 1024

bf16, f32 = jnp.bfloat16, jnp.float32


def tdot(a, b):
    return lax.dot_general(a, b, (((0,), (0,)), ((), ())), preferred_element_type=f32)


def ndot(a, b):
    return lax.dot_general(a, b, (((1,), (1,)), ((), ())), preferred_element_type=f32)


def swap(a, axis):
    return lax.all_to_all(a, axis, split_axis=0, concat_axis=0, tiled=True)


def across(a):
    return lax.ppermute(a, "core", [(0, 1), (1, 0)])


def cross(a, b):
    return (
        jnp.concatenate([a[:, :HALF], b[:, :HALF]], axis=1),
        jnp.concatenate([a[:, HALF:], b[:, HALF:]], axis=1),
    )


def tiles(width):
    per = width // (COLUMNS * 2 * LANES)
    for y in range(COLUMNS):
        for j in range(per):
            yield (y * per + j) * 2 * LANES, (y % PAIR) * PAIR, ((y // PAIR) * per + j) * LANES


def arrange(core_ref, gate_ref, up_ref, down_ref, keep_ref, send_ref):
    units = gate_ref.shape[0]

    def fill(pair_ref, single_ref):
        for at, place, to in tiles(gate_ref.shape[1]):
            a, b = slice(at, at + LANES), slice(at + LANES, at + 2 * LANES)
            for row, ref in ((0, gate_ref), (units, up_ref)):
                for zl, tile in enumerate(cross(ref[:, a], ref[:, b])):
                    pair_ref[place + zl, row:row + units, to:to + LANES] = tile
            for zl, tile in enumerate(cross(down_ref[:, a], down_ref[:, b])):
                single_ref[place + zl, 0:units, to:to + LANES] = tile
                single_ref[place + zl, units:2 * units, to:to + LANES] = tile

    @pl.when(core_ref[0] == 0)
    def _():
        fill(keep_ref, send_ref)

    @pl.when(core_ref[0] != 0)
    def _():
        fill(send_ref, keep_ref)


def join(keep_ref, recv_ref, out_ref):
    n = keep_ref.shape[1]
    for b in range(keep_ref.shape[0]):
        out_ref[b, :n] = keep_ref[b]
        out_ref[b, n:] = recv_ref[b]


def project(mine_ref, weights_ref, out_ref):
    n = weights_ref.shape[1] // 2
    for at in (0, n):
        total = ndot(mine_ref[0], weights_ref[0, at:at + n])
        for b in range(1, mine_ref.shape[0]):
            total = total + ndot(mine_ref[b], weights_ref[b, at:at + n])
        out_ref[:, at:at + n] = total


def activate(proj, dhid):
    units = dhid.shape[1]
    gate, upper = proj[:, :units], proj[:, units:]
    sig = jax.nn.sigmoid(gate)
    act = gate * sig
    hidden = (act * upper).astype(bf16)
    dgate = (dhid * upper * sig * (1.0 + gate * (1.0 - sig))).astype(bf16)
    dup = (dhid * act).astype(bf16)
    return hidden, jnp.concatenate([dgate, dup], axis=1)


def expand(core_ref, mine_ref, other_ref, weights_ref, part_ref):
    half = mine_ref.shape[1] // 2
    first = core_ref[0] == 0
    lefts = []
    for own, far in ((slice(0, half), slice(half, 2 * half)), (slice(half, 2 * half), slice(0, half))):
        here, there = mine_ref[:, own], other_ref[:, far]
        hidden, pair = activate(jnp.where(first, here, there), jnp.where(first, there, here)[:, :half // 2])
        lone = jnp.concatenate([hidden, jnp.zeros_like(hidden)], axis=1)
        lefts.append(jnp.where(first, pair.astype(f32), lone.astype(f32)).astype(bf16))
    left = jnp.concatenate(lefts, axis=1)
    for b in range(weights_ref.shape[0]):
        part_ref[b] = jnp.dot(left, weights_ref[b], preferred_element_type=f32).astype(bf16)


def weigh(core_ref, mine_ref, other_ref, here_ref, there_ref, gate_ref, up_ref, down_ref):
    units = gate_ref.shape[0]
    half = 2 * units

    def fill(rows_ref, cot_ref, proj, dhid):
        hidden, pair = activate(proj, dhid[:, :units])
        for at, place, to in tiles(gate_ref.shape[1]):
            both = []
            for ref in (rows_ref, cot_ref):
                both.append(jnp.concatenate(cross(ref[place, :, to:to + LANES], ref[place + 1, :, to:to + LANES]), axis=1))
            grads = tdot(pair, both[0]).astype(bf16)
            gate_ref[:, at:at + 2 * LANES] = grads[:units]
            up_ref[:, at:at + 2 * LANES] = grads[units:]
            down_ref[:, at:at + 2 * LANES] = tdot(hidden, both[1]).astype(bf16)

    here, there = here_ref[:, :half], there_ref[:, half:]

    @pl.when(core_ref[0] == 0)
    def _():
        fill(mine_ref, other_ref, here, there)

    @pl.when(core_ref[0] != 0)
    def _():
        fill(other_ref, mine_ref, there, here)


def turn(parts):
    n = len(parts)
    size = LANES // n
    group = lax.broadcasted_iota(jnp.int32, parts[0].shape, 1) // size
    outs = []
    for s in range(n):
        total = parts[s]
        for q in range(n):
            if q != s:
                total = jnp.where(group == q, pltpu.roll(parts[q], size * ((q - s) % n), 1), total)
        outs.append(total)
    return outs


def fan(tokens_ref, grad_ref, out_ref, both_ref, sem):
    copies = []
    for array, ref in enumerate((tokens_ref, grad_ref)):
        copies.append(pltpu.make_async_copy(ref, both_ref.at[array], sem.at[array]))
        copies[-1].start()
    for array, copy in enumerate(copies):
        copy.wait()
        rows = both_ref[array].astype(f32)
        lines = rows.shape[0] * rows.shape[1] // LANES
        pieces = [rows[at:at + lines] for at in range(0, rows.shape[0], lines)]
        packed = jnp.concatenate(pieces, axis=1).astype(bf16)
        for cell in range(out_ref.shape[0] // CORES):
            out_ref[cell * CORES + array] = packed


def dispatch(got_ref, pick_ref, weight_ref, out_ref):
    count = pick_ref.shape[1]
    lines = got_ref.shape[1]
    n = count // lines
    columns = []
    for g in range(got_ref.shape[0] // n):
        columns.append(jnp.concatenate(turn([got_ref[g * n + s].astype(f32) for s in range(n)]), axis=0))
    local = jnp.concatenate(columns, axis=1).astype(bf16)
    packed = jnp.dot(pick_ref[...], local, preferred_element_type=f32) * weight_ref[...]
    experts = pick_ref.shape[0] // SLOTS
    for e in range(experts):
        rows = packed[e * SLOTS:(e + 1) * SLOTS].astype(bf16)
        for b in range(out_ref.shape[0] // experts):
            out_ref[b * experts + e] = rows


def combine(got_ref, spread_ref, out_ref):
    experts = spread_ref.shape[1] // SLOTS
    sums = []
    for e in range(experts):
        total = got_ref[e].astype(f32)
        for b in range(1, got_ref.shape[0] // experts):
            total = total + got_ref[b * experts + e].astype(f32)
        sums.append(total)
    placed = lax.dot_general(
        spread_ref[...], jnp.concatenate(sums, axis=0), (((1,), (0,)), ((), ())),
        precision=lax.Precision.HIGHEST, preferred_element_type=f32,
    )
    lines = out_ref.shape[1]
    n = placed.shape[0] // lines
    for g in range(out_ref.shape[0] // n):
        column = placed[:, g * LANES:(g + 1) * LANES]
        for s, line in enumerate(turn([column[q * lines:(q + 1) * lines] for q in range(n)])):
            out_ref[g * n + s] = line.astype(bf16)


def finish(got_ref, back_ref, out_ref):
    for array, ref in enumerate((back_ref, out_ref)):
        total = got_ref[array].astype(f32)
        for cell in range(1, got_ref.shape[0] // CORES):
            total = total + got_ref[cell * CORES + array].astype(f32)
        narrow = ref.shape[1]
        pieces = [total[:, at:at + narrow] for at in range(0, LANES, narrow)]
        ref[...] = jnp.concatenate(pieces, axis=0).astype(bf16)


def kernel(body, outs, cost, core, *arrays, places=pltpu.VMEM, scratch=(), room=ROOM):
    specs = [pl.BlockSpec(memory_space=places)] * len(arrays)
    if core is not None:
        specs, arrays = [pl.BlockSpec(memory_space=pltpu.SMEM)] + specs, (core,) + arrays
    return pl.pallas_call(
        body,
        out_shape=tuple(jax.ShapeDtypeStruct(s, d) for s, d in outs),
        in_specs=specs,
        out_specs=tuple(pl.BlockSpec(memory_space=pltpu.VMEM) for _ in outs),
        scratch_shapes=list(scratch),
        compiler_params=pltpu.CompilerParams(vmem_limit_bytes=room),
        cost_estimate=pl.CostEstimate(flops=cost[0], bytes_accessed=cost[1], transcendentals=0),
        name=body.__name__,
    )(*arrays)


def on_device(tokens, routes, probs, w_gate, w_up, w_down, grad_out):
    experts = lax.axis_size("expert")
    cells = lax.axis_size("yh") * lax.axis_size("zh")
    near = PAIR * PAIR
    core = lax.axis_index("core")
    first = core == 0
    flag = core.astype(jnp.int32).reshape(1)
    count, narrow = tokens.shape
    wide = cells * CORES * narrow
    rows_of = experts * SLOTS
    units, width = w_gate.shape[1:]

    labels = lax.broadcasted_iota(jnp.int32, (experts, count, routes.shape[1]), 0)
    hits = routes[None] == labels
    mask = jnp.any(hits, axis=2)
    share = jnp.sum(jnp.where(hits, probs[None], 0.0), axis=2)
    earlier = lax.broadcasted_iota(jnp.int32, (count, count), 1) < lax.broadcasted_iota(jnp.int32, (count, count), 0)
    place = jnp.sum(jnp.where(earlier[None] & mask[:, None, :], 1, 0), axis=2)
    slots = lax.broadcasted_iota(jnp.int32, (experts, SLOTS, count), 1)
    chosen = (place[:, None, :] == slots) & mask[:, None, :]
    pick = chosen.reshape(rows_of, count).astype(bf16)
    weight = jnp.where(first, jnp.ones_like(share), share)
    slot_weight = jnp.sum(jnp.where(chosen, weight[:, None, :], 0.0), axis=2).reshape(rows_of, 1)

    lines = count * narrow // LANES
    small = 2 * cells * CORES * count * narrow
    (sent,) = kernel(
        fan, [((cells * CORES, lines, LANES), bf16)], (0, small), None, tokens, grad_out, places=pltpu.HBM,
        scratch=[pltpu.VMEM((2, count, narrow), bf16), pltpu.SemaphoreType.DMA((2,))], room=ALL,
    )
    got = swap(sent, ("yh", "zh", "core"))

    big = 2 * units * width
    keep, send = kernel(
        arrange, [((near, 2 * units, wide), bf16)] * 2, (0, 8 * big), flag, w_gate[0], w_up[0], w_down[0]
    )
    (weights,) = kernel(join, [((near, 4 * units, wide), bf16)], (0, 8 * big), None, keep, across(send))

    block = ((near * experts, SLOTS, wide), bf16)
    (sent,) = kernel(dispatch, [block], (0, 2 * near * rows_of * wide), None, got, pick, slot_weight)
    got = swap(sent, ("yl", "zl", "expert"))
    mine = got.reshape(near, rows_of, wide)

    work = 2 * rows_of * 2 * big
    (proj,) = kernel(project, [((rows_of, 4 * units), f32)], (work, 6 * big), None, mine, weights)
    other = across(proj)
    (part,) = kernel(expand, [((near, rows_of, wide), bf16)], (work, 6 * big), flag, proj, other, weights)

    mine, part = lax.optimization_barrier((mine, part))
    grad_gate, grad_up, grad_down = kernel(
        weigh, [((units, width), bf16)] * 3, (work, 8 * big), flag, mine, across(mine), proj, other
    )
    got = swap(part.reshape(near * experts, SLOTS, wide), ("yl", "zl", "expert"))
    got, grad_gate, grad_up, grad_down = lax.optimization_barrier((got, grad_gate, grad_up, grad_down))
    back_weight = jnp.where(first, mask.astype(f32), share)
    spread = jnp.where(chosen, back_weight[:, None, :], 0.0).reshape(rows_of, count).T
    (sent,) = kernel(
        combine, [((cells * CORES, lines, LANES), bf16)], (0, 2 * near * rows_of * wide), None, got, spread
    )
    got = swap(sent, ("yh", "zh", "core"))
    grad_tokens, mixed = kernel(finish, [((count, narrow), bf16)] * 2, (0, small), None, got)

    return (mixed, grad_tokens, grad_gate[None], grad_up[None], grad_down[None])


def solution(mesh):
    dp, experts = mesh.devices.shape
    depth = dp // (COLUMNS * CORES)
    split = mesh.devices.reshape(COLUMNS // PAIR, PAIR, depth // PAIR, PAIR, CORES, experts)
    fine = Mesh(split, ("yh", "yl", "zh", "zl", "core", "expert"))
    dp = ("yh", "yl", "zh", "zl", "core")
    placed = (
        P("expert", dp),
        P("expert", None),
        P("expert", None),
        P("expert", dp, None),
        P("expert", dp, None),
        P("expert", dp, None),
        P("expert", dp),
    )
    return jax.shard_map(
        on_device,
        mesh=fine,
        in_specs=placed,
        out_specs=(P("expert", dp), P("expert", dp), P("expert", dp, None), P("expert", dp, None), P("expert", dp, None)),
        check_vma=False,
    )
```

```python
import jax
import jax.numpy as jnp
from jax import lax
from jax.experimental import pallas as pl
from jax.experimental.pallas import tpu as pltpu
from jax.sharding import Mesh, PartitionSpec as P

CORES = 2
COLUMNS = 8
PAIR = 2
SLOTS = 24
HALF = 64
LANES = 128
ROOM = 16 * 1024 * 1024
ALL = 60 * 1024 * 1024

bf16, f32 = jnp.bfloat16, jnp.float32


def tdot(a, b):
    return lax.dot_general(a, b, (((0,), (0,)), ((), ())), preferred_element_type=f32)


def ndot(a, b):
    return lax.dot_general(a, b, (((1,), (1,)), ((), ())), preferred_element_type=f32)


def swap(a, axis):
    return lax.all_to_all(a, axis, split_axis=0, concat_axis=0, tiled=True)


def across(a):
    return lax.ppermute(a, "core", [(0, 1), (1, 0)])


def cross(a, b):
    return (
        jnp.concatenate([a[:, :HALF], b[:, :HALF]], axis=1),
        jnp.concatenate([a[:, HALF:], b[:, HALF:]], axis=1),
    )


def tiles(width):
    per = width // (COLUMNS * 2 * LANES)
    for y in range(COLUMNS):
        for j in range(per):
            yield (y * per + j) * 2 * LANES, (y % PAIR) * PAIR, ((y // PAIR) * per + j) * LANES


def arrange(core_ref, gate_ref, up_ref, down_ref, keep_ref, send_ref):
    units = gate_ref.shape[0]

    def fill(pair_ref, single_ref):
        for at, place, to in tiles(gate_ref.shape[1]):
            a, b = slice(at, at + LANES), slice(at + LANES, at + 2 * LANES)
            for row, ref in ((0, gate_ref), (units, up_ref)):
                for zl, tile in enumerate(cross(ref[:, a], ref[:, b])):
                    pair_ref[place + zl, row:row + units, to:to + LANES] = tile
            for zl, tile in enumerate(cross(down_ref[:, a], down_ref[:, b])):
                single_ref[place + zl, 0:units, to:to + LANES] = tile
                single_ref[place + zl, units:2 * units, to:to + LANES] = tile

    @pl.when(core_ref[0] == 0)
    def _():
        fill(keep_ref, send_ref)

    @pl.when(core_ref[0] != 0)
    def _():
        fill(send_ref, keep_ref)


def settle(recv_ref, out_ref):
    for b in range(recv_ref.shape[0]):
        out_ref[b] = recv_ref[b]


def product(mine_ref, weights_ref):
    total = ndot(mine_ref[0], weights_ref[0])
    for b in range(1, mine_ref.shape[0]):
        total = total + ndot(mine_ref[b], weights_ref[b])
    return total


def project_own(mine_ref, keep_ref, out_ref):
    out_ref[...] = product(mine_ref, keep_ref)


def project_far(own_ref, mine_ref, far_ref, out_ref):
    n = own_ref.shape[1]
    out_ref[:, :n] = own_ref[...]
    out_ref[:, n:] = product(mine_ref, far_ref)


def activate(proj, dhid):
    units = dhid.shape[1]
    gate, upper = proj[:, :units], proj[:, units:]
    sig = jax.nn.sigmoid(gate)
    act = gate * sig
    hidden = (act * upper).astype(bf16)
    dgate = (dhid * upper * sig * (1.0 + gate * (1.0 - sig))).astype(bf16)
    dup = (dhid * act).astype(bf16)
    return hidden, jnp.concatenate([dgate, dup], axis=1)


def expand(core_ref, mine_ref, other_ref, keep_ref, far_ref, part_ref):
    half = mine_ref.shape[1] // 2
    first = core_ref[0] == 0
    lefts = []
    for own, far in ((slice(0, half), slice(half, 2 * half)), (slice(half, 2 * half), slice(0, half))):
        here, there = mine_ref[:, own], other_ref[:, far]
        hidden, pair = activate(jnp.where(first, here, there), jnp.where(first, there, here)[:, :half // 2])
        lone = jnp.concatenate([hidden, jnp.zeros_like(hidden)], axis=1)
        lefts.append(jnp.where(first, pair.astype(f32), lone.astype(f32)).astype(bf16))
    for b in range(keep_ref.shape[0]):
        total = jnp.dot(lefts[0], keep_ref[b], preferred_element_type=f32)
        part_ref[b] = (total + jnp.dot(lefts[1], far_ref[b], preferred_element_type=f32)).astype(bf16)


def weigh(core_ref, mine_ref, other_ref, here_ref, there_ref, gate_ref, up_ref, down_ref):
    units = gate_ref.shape[0]
    half = 2 * units

    def fill(rows_ref, cot_ref, proj, dhid):
        hidden, pair = activate(proj, dhid[:, :units])
        for at, place, to in tiles(gate_ref.shape[1]):
            both = []
            for ref in (rows_ref, cot_ref):
                both.append(jnp.concatenate(cross(ref[place, :, to:to + LANES], ref[place + 1, :, to:to + LANES]), axis=1))
            grads = tdot(pair, both[0]).astype(bf16)
            gate_ref[:, at:at + 2 * LANES] = grads[:units]
            up_ref[:, at:at + 2 * LANES] = grads[units:]
            down_ref[:, at:at + 2 * LANES] = tdot(hidden, both[1]).astype(bf16)

    here, there = here_ref[:, :half], there_ref[:, half:]

    @pl.when(core_ref[0] == 0)
    def _():
        fill(mine_ref, other_ref, here, there)

    @pl.when(core_ref[0] != 0)
    def _():
        fill(other_ref, mine_ref, there, here)


def turn(parts):
    n = len(parts)
    size = LANES // n
    group = lax.broadcasted_iota(jnp.int32, parts[0].shape, 1) // size
    outs = []
    for s in range(n):
        total = parts[s]
        for q in range(n):
            if q != s:
                total = jnp.where(group == q, pltpu.roll(parts[q], size * ((q - s) % n), 1), total)
        outs.append(total)
    return outs


def fan(tokens_ref, grad_ref, out_ref, both_ref, sem):
    copies = []
    for array, ref in enumerate((tokens_ref, grad_ref)):
        copies.append(pltpu.make_async_copy(ref, both_ref.at[array], sem.at[array]))
        copies[-1].start()
    for array, copy in enumerate(copies):
        copy.wait()
        rows = both_ref[array].astype(f32)
        lines = rows.shape[0] * rows.shape[1] // LANES
        pieces = [rows[at:at + lines] for at in range(0, rows.shape[0], lines)]
        packed = jnp.concatenate(pieces, axis=1).astype(bf16)
        for cell in range(out_ref.shape[0] // CORES):
            out_ref[cell * CORES + array] = packed


def dispatch(got_ref, pick_ref, weight_ref, out_ref):
    count = pick_ref.shape[1]
    lines = got_ref.shape[1]
    n = count // lines
    columns = []
    for g in range(got_ref.shape[0] // n):
        columns.append(jnp.concatenate(turn([got_ref[g * n + s].astype(f32) for s in range(n)]), axis=0))
    local = jnp.concatenate(columns, axis=1).astype(bf16)
    packed = jnp.dot(pick_ref[...], local, preferred_element_type=f32) * weight_ref[...]
    experts = pick_ref.shape[0] // SLOTS
    for e in range(experts):
        rows = packed[e * SLOTS:(e + 1) * SLOTS].astype(bf16)
        for b in range(out_ref.shape[0] // experts):
            out_ref[b * experts + e] = rows


def combine(got_ref, spread_ref, out_ref):
    experts = spread_ref.shape[1] // SLOTS
    sums = []
    for e in range(experts):
        total = got_ref[e].astype(f32)
        for b in range(1, got_ref.shape[0] // experts):
            total = total + got_ref[b * experts + e].astype(f32)
        sums.append(total)
    placed = lax.dot_general(
        spread_ref[...], jnp.concatenate(sums, axis=0), (((1,), (0,)), ((), ())),
        precision=lax.Precision.HIGHEST, preferred_element_type=f32,
    )
    lines = out_ref.shape[1]
    n = placed.shape[0] // lines
    for g in range(out_ref.shape[0] // n):
        column = placed[:, g * LANES:(g + 1) * LANES]
        for s, line in enumerate(turn([column[q * lines:(q + 1) * lines] for q in range(n)])):
            out_ref[g * n + s] = line.astype(bf16)


def finish(got_ref, back_ref, out_ref):
    for array, ref in enumerate((back_ref, out_ref)):
        total = got_ref[array].astype(f32)
        for cell in range(1, got_ref.shape[0] // CORES):
            total = total + got_ref[cell * CORES + array].astype(f32)
        narrow = ref.shape[1]
        pieces = [total[:, at:at + narrow] for at in range(0, LANES, narrow)]
        ref[...] = jnp.concatenate(pieces, axis=0).astype(bf16)


def kernel(body, outs, cost, core, *arrays, places=pltpu.VMEM, scratch=(), room=ROOM):
    specs = [pl.BlockSpec(memory_space=places)] * len(arrays)
    if core is not None:
        specs, arrays = [pl.BlockSpec(memory_space=pltpu.SMEM)] + specs, (core,) + arrays
    return pl.pallas_call(
        body,
        out_shape=tuple(jax.ShapeDtypeStruct(s, d) for s, d in outs),
        in_specs=specs,
        out_specs=tuple(pl.BlockSpec(memory_space=pltpu.VMEM) for _ in outs),
        scratch_shapes=list(scratch),
        compiler_params=pltpu.CompilerParams(vmem_limit_bytes=room),
        cost_estimate=pl.CostEstimate(flops=cost[0], bytes_accessed=cost[1], transcendentals=0),
        name=body.__name__,
    )(*arrays)


def on_device(tokens, routes, probs, w_gate, w_up, w_down, grad_out):
    experts = lax.axis_size("expert")
    cells = lax.axis_size("yh") * lax.axis_size("zh")
    near = PAIR * PAIR
    core = lax.axis_index("core")
    first = core == 0
    flag = core.astype(jnp.int32).reshape(1)
    count, narrow = tokens.shape
    wide = cells * CORES * narrow
    rows_of = experts * SLOTS
    units, width = w_gate.shape[1:]

    labels = lax.broadcasted_iota(jnp.int32, (experts, count, routes.shape[1]), 0)
    hits = routes[None] == labels
    mask = jnp.any(hits, axis=2)
    share = jnp.sum(jnp.where(hits, probs[None], 0.0), axis=2)
    earlier = lax.broadcasted_iota(jnp.int32, (count, count), 1) < lax.broadcasted_iota(jnp.int32, (count, count), 0)
    place = jnp.sum(jnp.where(earlier[None] & mask[:, None, :], 1, 0), axis=2)
    slots = lax.broadcasted_iota(jnp.int32, (experts, SLOTS, count), 1)
    chosen = (place[:, None, :] == slots) & mask[:, None, :]
    pick = chosen.reshape(rows_of, count).astype(bf16)
    weight = jnp.where(first, jnp.ones_like(share), share)
    slot_weight = jnp.sum(jnp.where(chosen, weight[:, None, :], 0.0), axis=2).reshape(rows_of, 1)

    lines = count * narrow // LANES
    small = 2 * cells * CORES * count * narrow
    (sent,) = kernel(
        fan, [((cells * CORES, lines, LANES), bf16)], (0, small), None, tokens, grad_out, places=pltpu.HBM,
        scratch=[pltpu.VMEM((2, count, narrow), bf16), pltpu.SemaphoreType.DMA((2,))], room=ALL,
    )
    got = swap(sent, ("yh", "zh", "core"))

    big = 2 * units * width
    keep, send = kernel(
        arrange, [((near, 2 * units, wide), bf16)] * 2, (0, 8 * big), flag, w_gate[0], w_up[0], w_down[0]
    )
    (far,) = kernel(settle, [((near, 2 * units, wide), bf16)], (0, 4 * big), None, across(send))

    block = ((near * experts, SLOTS, wide), bf16)
    (sent,) = kernel(dispatch, [block], (0, 2 * near * rows_of * wide), None, got, pick, slot_weight)
    got = swap(sent, ("yl", "zl", "expert"))
    mine = got.reshape(near, rows_of, wide)

    work = 2 * rows_of * 2 * big
    (own,) = kernel(project_own, [((rows_of, 2 * units), f32)], (work // 2, 3 * big), None, mine, keep)
    (proj,) = kernel(project_far, [((rows_of, 4 * units), f32)], (work // 2, 3 * big), None, own, mine, far)
    other = across(proj)
    (part,) = kernel(expand, [((near, rows_of, wide), bf16)], (work, 6 * big), flag, proj, other, keep, far)

    mine, part = lax.optimization_barrier((mine, part))
    grad_gate, grad_up, grad_down = kernel(
        weigh, [((units, width), bf16)] * 3, (work, 8 * big), flag, mine, across(mine), proj, other
    )
    got = swap(part.reshape(near * experts, SLOTS, wide), ("yl", "zl", "expert"))
    got, grad_gate, grad_up, grad_down = lax.optimization_barrier((got, grad_gate, grad_up, grad_down))
    back_weight = jnp.where(first, mask.astype(f32), share)
    spread = jnp.where(chosen, back_weight[:, None, :], 0.0).reshape(rows_of, count).T
    (sent,) = kernel(
        combine, [((cells * CORES, lines, LANES), bf16)], (0, 2 * near * rows_of * wide), None, got, spread
    )
    got = swap(sent, ("yh", "zh", "core"))
    grad_tokens, mixed = kernel(finish, [((count, narrow), bf16)] * 2, (0, small), None, got)

    return (mixed, grad_tokens, grad_gate[None], grad_up[None], grad_down[None])


def solution(mesh):
    dp, experts = mesh.devices.shape
    depth = dp // (COLUMNS * CORES)
    split = mesh.devices.reshape(COLUMNS // PAIR, PAIR, depth // PAIR, PAIR, CORES, experts)
    fine = Mesh(split, ("yh", "yl", "zh", "zl", "core", "expert"))
    dp = ("yh", "yl", "zh", "zl", "core")
    placed = (
        P("expert", dp),
        P("expert", None),
        P("expert", None),
        P("expert", dp, None),
        P("expert", dp, None),
        P("expert", dp, None),
        P("expert", dp),
    )
    return jax.shard_map(
        on_device,
        mesh=fine,
        in_specs=placed,
        out_specs=(P("expert", dp), P("expert", dp), P("expert", dp, None), P("expert", dp, None), P("expert", dp, None)),
        check_vma=False,
    )
```

```python
import jax
import jax.numpy as jnp
from jax import lax
from jax.experimental import pallas as pl
from jax.experimental.pallas import tpu as pltpu
from jax.sharding import Mesh, PartitionSpec as P

CORES = 2
COLUMNS = 8
PAIR = 2
SLOTS = 24
HALF = 64
LANES = 128
ROOM = 16 * 1024 * 1024
ALL = 60 * 1024 * 1024

bf16, f32 = jnp.bfloat16, jnp.float32


def tdot(a, b):
    return lax.dot_general(a, b, (((0,), (0,)), ((), ())), preferred_element_type=f32)


def ndot(a, b):
    return lax.dot_general(a, b, (((1,), (1,)), ((), ())), preferred_element_type=f32)


def swap(a, axis):
    return lax.all_to_all(a, axis, split_axis=0, concat_axis=0, tiled=True)


def across(a):
    return lax.ppermute(a, "core", [(0, 1), (1, 0)])


def cross(a, b):
    return (
        jnp.concatenate([a[:, :HALF], b[:, :HALF]], axis=1),
        jnp.concatenate([a[:, HALF:], b[:, HALF:]], axis=1),
    )


def tiles(width):
    per = width // (COLUMNS * 2 * LANES)
    for y in range(COLUMNS):
        for j in range(per):
            yield (y * per + j) * 2 * LANES, (y % PAIR) * PAIR, ((y // PAIR) * per + j) * LANES


def arrange(core_ref, gate_ref, up_ref, down_ref, keep_ref, send_ref):
    units = gate_ref.shape[0]

    def fill(pair_ref, single_ref):
        for at, place, to in tiles(gate_ref.shape[1]):
            a, b = slice(at, at + LANES), slice(at + LANES, at + 2 * LANES)
            for row, ref in ((0, gate_ref), (units, up_ref)):
                for zl, tile in enumerate(cross(ref[:, a], ref[:, b])):
                    pair_ref[place + zl, row:row + units, to:to + LANES] = tile
            for zl, tile in enumerate(cross(down_ref[:, a], down_ref[:, b])):
                single_ref[place + zl, 0:units, to:to + LANES] = tile
                single_ref[place + zl, units:2 * units, to:to + LANES] = tile

    @pl.when(core_ref[0] == 0)
    def _():
        fill(keep_ref, send_ref)

    @pl.when(core_ref[0] != 0)
    def _():
        fill(send_ref, keep_ref)


def join(keep_ref, recv_ref, out_ref):
    n = keep_ref.shape[1]
    for b in range(keep_ref.shape[0]):
        out_ref[b, :n] = keep_ref[b]
        out_ref[b, n:] = recv_ref[b]


def project(mine_ref, weights_ref, out_ref, rows_ref):
    for b in range(mine_ref.shape[0]):
        rows_ref[b] = mine_ref[b]
    n = weights_ref.shape[1] // 2
    for at in (0, n):
        total = ndot(mine_ref[0], weights_ref[0, at:at + n])
        for b in range(1, mine_ref.shape[0]):
            total = total + ndot(mine_ref[b], weights_ref[b, at:at + n])
        out_ref[:, at:at + n] = total


def activate(proj, dhid):
    units = dhid.shape[1]
    gate, upper = proj[:, :units], proj[:, units:]
    sig = jax.nn.sigmoid(gate)
    act = gate * sig
    hidden = (act * upper).astype(bf16)
    dgate = (dhid * upper * sig * (1.0 + gate * (1.0 - sig))).astype(bf16)
    dup = (dhid * act).astype(bf16)
    return hidden, jnp.concatenate([dgate, dup], axis=1)


def expand(core_ref, mine_ref, other_ref, weights_ref, part_ref):
    half = mine_ref.shape[1] // 2
    first = core_ref[0] == 0
    lefts = []
    for own, far in ((slice(0, half), slice(half, 2 * half)), (slice(half, 2 * half), slice(0, half))):
        here, there = mine_ref[:, own], other_ref[:, far]
        hidden, pair = activate(jnp.where(first, here, there), jnp.where(first, there, here)[:, :half // 2])
        lone = jnp.concatenate([hidden, jnp.zeros_like(hidden)], axis=1)
        lefts.append(jnp.where(first, pair.astype(f32), lone.astype(f32)).astype(bf16))
    left = jnp.concatenate(lefts, axis=1)
    for b in range(weights_ref.shape[0]):
        part_ref[b] = jnp.dot(left, weights_ref[b], preferred_element_type=f32).astype(bf16)


def weigh(core_ref, mine_ref, other_ref, here_ref, there_ref, gate_ref, up_ref, down_ref):
    units = gate_ref.shape[0]
    half = 2 * units

    def fill(rows_ref, cot_ref, proj, dhid):
        hidden, pair = activate(proj, dhid[:, :units])
        for at, place, to in tiles(gate_ref.shape[1]):
            both = []
            for ref in (rows_ref, cot_ref):
                both.append(jnp.concatenate(cross(ref[place, :, to:to + LANES], ref[place + 1, :, to:to + LANES]), axis=1))
            grads = tdot(pair, both[0]).astype(bf16)
            gate_ref[:, at:at + 2 * LANES] = grads[:units]
            up_ref[:, at:at + 2 * LANES] = grads[units:]
            down_ref[:, at:at + 2 * LANES] = tdot(hidden, both[1]).astype(bf16)

    here, there = here_ref[:, :half], there_ref[:, half:]

    @pl.when(core_ref[0] == 0)
    def _():
        fill(mine_ref, other_ref, here, there)

    @pl.when(core_ref[0] != 0)
    def _():
        fill(other_ref, mine_ref, there, here)


def turn(parts):
    n = len(parts)
    size = LANES // n
    group = lax.broadcasted_iota(jnp.int32, parts[0].shape, 1) // size
    outs = []
    for s in range(n):
        total = parts[s]
        for q in range(n):
            if q != s:
                total = jnp.where(group == q, pltpu.roll(parts[q], size * ((q - s) % n), 1), total)
        outs.append(total)
    return outs


def fan(tokens_ref, grad_ref, out_ref, both_ref, sem):
    copies = []
    for array, ref in enumerate((tokens_ref, grad_ref)):
        copies.append(pltpu.make_async_copy(ref, both_ref.at[array], sem.at[array]))
        copies[-1].start()
    for array, copy in enumerate(copies):
        copy.wait()
        rows = both_ref[array].astype(f32)
        lines = rows.shape[0] * rows.shape[1] // LANES
        pieces = [rows[at:at + lines] for at in range(0, rows.shape[0], lines)]
        packed = jnp.concatenate(pieces, axis=1).astype(bf16)
        for cell in range(out_ref.shape[0] // CORES):
            out_ref[cell * CORES + array] = packed


def dispatch(got_ref, pick_ref, weight_ref, out_ref):
    count = pick_ref.shape[1]
    lines = got_ref.shape[1]
    n = count // lines
    columns = []
    for g in range(got_ref.shape[0] // n):
        columns.append(jnp.concatenate(turn([got_ref[g * n + s].astype(f32) for s in range(n)]), axis=0))
    local = jnp.concatenate(columns, axis=1).astype(bf16)
    packed = jnp.dot(pick_ref[...], local, preferred_element_type=f32) * weight_ref[...]
    experts = pick_ref.shape[0] // SLOTS
    for e in range(experts):
        rows = packed[e * SLOTS:(e + 1) * SLOTS].astype(bf16)
        for b in range(out_ref.shape[0] // experts):
            out_ref[b * experts + e] = rows


def combine(got_ref, spread_ref, out_ref):
    experts = spread_ref.shape[1] // SLOTS
    sums = []
    for e in range(experts):
        total = got_ref[e].astype(f32)
        for b in range(1, got_ref.shape[0] // experts):
            total = total + got_ref[b * experts + e].astype(f32)
        sums.append(total)
    placed = lax.dot_general(
        spread_ref[...], jnp.concatenate(sums, axis=0), (((1,), (0,)), ((), ())),
        precision=lax.Precision.HIGHEST, preferred_element_type=f32,
    )
    lines = out_ref.shape[1]
    n = placed.shape[0] // lines
    for g in range(out_ref.shape[0] // n):
        column = placed[:, g * LANES:(g + 1) * LANES]
        for s, line in enumerate(turn([column[q * lines:(q + 1) * lines] for q in range(n)])):
            out_ref[g * n + s] = line.astype(bf16)


def finish(got_ref, back_ref, out_ref):
    for array, ref in enumerate((back_ref, out_ref)):
        total = got_ref[array].astype(f32)
        for cell in range(1, got_ref.shape[0] // CORES):
            total = total + got_ref[cell * CORES + array].astype(f32)
        narrow = ref.shape[1]
        pieces = [total[:, at:at + narrow] for at in range(0, LANES, narrow)]
        ref[...] = jnp.concatenate(pieces, axis=0).astype(bf16)


def kernel(body, outs, cost, core, *arrays, places=pltpu.VMEM, scratch=(), room=ROOM):
    specs = [pl.BlockSpec(memory_space=places)] * len(arrays)
    if core is not None:
        specs, arrays = [pl.BlockSpec(memory_space=pltpu.SMEM)] + specs, (core,) + arrays
    return pl.pallas_call(
        body,
        out_shape=tuple(jax.ShapeDtypeStruct(s, d) for s, d in outs),
        in_specs=specs,
        out_specs=tuple(pl.BlockSpec(memory_space=pltpu.VMEM) for _ in outs),
        scratch_shapes=list(scratch),
        compiler_params=pltpu.CompilerParams(vmem_limit_bytes=room),
        cost_estimate=pl.CostEstimate(flops=cost[0], bytes_accessed=cost[1], transcendentals=0),
        name=body.__name__,
    )(*arrays)


def on_device(tokens, routes, probs, w_gate, w_up, w_down, grad_out):
    experts = lax.axis_size("expert")
    cells = lax.axis_size("yh") * lax.axis_size("zh")
    near = PAIR * PAIR
    core = lax.axis_index("core")
    first = core == 0
    flag = core.astype(jnp.int32).reshape(1)
    count, narrow = tokens.shape
    wide = cells * CORES * narrow
    rows_of = experts * SLOTS
    units, width = w_gate.shape[1:]

    labels = lax.broadcasted_iota(jnp.int32, (experts, count, routes.shape[1]), 0)
    hits = routes[None] == labels
    mask = jnp.any(hits, axis=2)
    share = jnp.sum(jnp.where(hits, probs[None], 0.0), axis=2)
    earlier = lax.broadcasted_iota(jnp.int32, (count, count), 1) < lax.broadcasted_iota(jnp.int32, (count, count), 0)
    place = jnp.sum(jnp.where(earlier[None] & mask[:, None, :], 1, 0), axis=2)
    slots = lax.broadcasted_iota(jnp.int32, (experts, SLOTS, count), 1)
    chosen = (place[:, None, :] == slots) & mask[:, None, :]
    pick = chosen.reshape(rows_of, count).astype(bf16)
    weight = jnp.where(first, jnp.ones_like(share), share)
    slot_weight = jnp.sum(jnp.where(chosen, weight[:, None, :], 0.0), axis=2).reshape(rows_of, 1)

    lines = count * narrow // LANES
    small = 2 * cells * CORES * count * narrow
    (sent,) = kernel(
        fan, [((cells * CORES, lines, LANES), bf16)], (0, small), None, tokens, grad_out, places=pltpu.HBM,
        scratch=[pltpu.VMEM((2, count, narrow), bf16), pltpu.SemaphoreType.DMA((2,))], room=ALL,
    )
    got = swap(sent, ("yh", "zh", "core"))

    big = 2 * units * width
    keep, send = kernel(
        arrange, [((near, 2 * units, wide), bf16)] * 2, (0, 8 * big), flag, w_gate[0], w_up[0], w_down[0]
    )
    (weights,) = kernel(join, [((near, 4 * units, wide), bf16)], (0, 8 * big), None, keep, across(send))

    block = ((near * experts, SLOTS, wide), bf16)
    (sent,) = kernel(dispatch, [block], (0, 2 * near * rows_of * wide), None, got, pick, slot_weight)
    got = swap(sent, ("yl", "zl", "expert"))
    mine = got.reshape(near, rows_of, wide)

    work = 2 * rows_of * 2 * big
    outs = [((rows_of, 4 * units), f32), ((near, rows_of, wide), bf16)]
    proj, mine = kernel(project, outs, (work, 6 * big), None, mine, weights)
    other = across(proj)
    (part,) = kernel(expand, [((near, rows_of, wide), bf16)], (work, 6 * big), flag, proj, other, weights)

    mine, part = lax.optimization_barrier((mine, part))
    grad_gate, grad_up, grad_down = kernel(
        weigh, [((units, width), bf16)] * 3, (work, 8 * big), flag, mine, across(mine), proj, other
    )
    got = swap(part.reshape(near * experts, SLOTS, wide), ("yl", "zl", "expert"))
    got, grad_gate, grad_up, grad_down = lax.optimization_barrier((got, grad_gate, grad_up, grad_down))
    back_weight = jnp.where(first, mask.astype(f32), share)
    spread = jnp.where(chosen, back_weight[:, None, :], 0.0).reshape(rows_of, count).T
    (sent,) = kernel(
        combine, [((cells * CORES, lines, LANES), bf16)], (0, 2 * near * rows_of * wide), None, got, spread
    )
    got = swap(sent, ("yh", "zh", "core"))
    grad_tokens, mixed = kernel(finish, [((count, narrow), bf16)] * 2, (0, small), None, got)

    return (mixed, grad_tokens, grad_gate[None], grad_up[None], grad_down[None])


def solution(mesh):
    dp, experts = mesh.devices.shape
    depth = dp // (COLUMNS * CORES)
    split = mesh.devices.reshape(COLUMNS // PAIR, PAIR, depth // PAIR, PAIR, CORES, experts)
    fine = Mesh(split, ("yh", "yl", "zh", "zl", "core", "expert"))
    dp = ("yh", "yl", "zh", "zl", "core")
    placed = (
        P("expert", dp),
        P("expert", None),
        P("expert", None),
        P("expert", dp, None),
        P("expert", dp, None),
        P("expert", dp, None),
        P("expert", dp),
    )
    return jax.shard_map(
        on_device,
        mesh=fine,
        in_specs=placed,
        out_specs=(P("expert", dp), P("expert", dp), P("expert", dp, None), P("expert", dp, None), P("expert", dp, None)),
        check_vma=False,
    )
```
